256 devices in a mesh: dp: 32 (over y, x, core), tensor: 8 (over z).
Axes of the slice: x: 4, y: 4, z: 8, core: 2. Of those that a mesh axis runs over, the one named last changes fastest.
Arguments:
- queries: bfloat16 [32768, 4096], P(('dp', 'tensor')), may hold values from -170 to 170
- keys: bfloat16 [32768, 1024], P(('dp', 'tensor')), may hold values from -7 to 7
- values: bfloat16 [32768, 1024], P(('dp', 'tensor')), may hold values from -6 to 6
- grad_out: bfloat16 [32768, 4096], P(('dp', 'tensor')), may hold values from -12 to 12
- chosen_len: int32 [128], replicated, may hold values from 16 to 240
- pack_of: int32 [128], replicated, may hold values from 0 to 31, as said below
- pack_offset: int32 [128], replicated, may hold values from 0 to 768, as said below
Outputs:
- grad_queries: bfloat16 [32768, 4096], P(('dp', 'tensor'))
- grad_keys: bfloat16 [32768, 1024], P(('dp', 'tensor'))
- grad_values: bfloat16 [32768, 1024], P(('dp', 'tensor'))
The draws below stay inside these ranges and needn't reach their ends.
Inputs may be any that keep to these rules, and one draw needn't show every extreme that they name: `pack_of`: every pack receives exactly 4 pairs; the 4 consecutive pairs of one loader shard go to 4 different packs, one pair to each. `pack_offset`: within one pack the offsets of its pairs are the multiples of 256 below 1024, each once.
All inputs are finite; a program needn't handle non-finite values.
Results may differ from the reference program's by a relative error of at most 0.011.
Values may be sent and summed in bfloat16 or wider, within the bound.
No kernel may reach another device: no remote copies, remote signals or barrier semaphores. Data moves between devices by JAX's collectives and lax.ppermute only.
A program may use at most 128 MiB of HBM per device.

```python
import math
import jax
import jax.numpy as jnp
from jax import lax

QUERY_HEAD_COUNT = 32
KEY_VALUE_HEADS = 8
HEAD_WIDTH = 128
PAIR_TOKENS = 256
QUERY_PER_KEY = 4
PACK = 1024
PAIRS = 128
TOTAL_TOKENS = 32768
N_DP = 32


def base_keys(key):
    return jax.random.truncated_normal(key, -6.0, 6.0, (TOTAL_TOKENS, KEY_VALUE_HEADS * HEAD_WIDTH), jnp.float32)


def pack_plan(key):
    per_shard = PACK // PAIR_TOKENS
    orders = jax.random.permutation(jax.random.fold_in(key, 101), N_DP)
    offsets = jax.random.permutation(jax.random.fold_in(key, 102), per_shard) % N_DP
    shard_ids = jnp.arange(N_DP)[:, None]
    targets = orders[(shard_ids + offsets[None, :]) % N_DP]
    return targets.reshape(-1).astype(jnp.int32)


def draw_keys(key, part):
    return base_keys(key).astype(jnp.bfloat16)


def draw_queries(key, part):
    key = jax.random.fold_in(key, 11)
    return jax.random.truncated_normal(key, -6.0, 6.0, (TOTAL_TOKENS, QUERY_HEAD_COUNT * HEAD_WIDTH), jnp.float32).astype(jnp.bfloat16)


def draw_pack_of(key, part):
    targets = pack_plan(key)
    return targets


def draw_pack_offset(key, part):
    targets = pack_plan(key)
    key = jax.random.fold_in(key, 9)
    per_shard = PACK // PAIR_TOKENS
    pack_keys = jax.random.split(key, N_DP)
    slot_table = jax.vmap(lambda single: jax.random.permutation(single, per_shard))(pack_keys)
    column = jnp.arange(N_DP * per_shard) % per_shard
    return (slot_table[targets, column] * PAIR_TOKENS).astype(jnp.int32)


def touch_ends(entries, own_key, least, high):
    index_at = [jax.random.randint(jax.random.fold_in(own_key, axis), (), 0, length) for axis, length in enumerate(entries.shape)]
    widest = entries.shape.index(max(entries.shape))
    neighbour = index_at[:widest] + [(index_at[widest] + 1) % entries.shape[widest]] + index_at[widest + 1:]
    return entries.at[tuple(index_at)].set(least).at[tuple(neighbour)].set(high)


def level_of(key, dims, cuts, smallest, high):
    level, own = 1.0, jax.random.fold_in(key, 6)
    for dim, blocks in cuts:
        draws = jnp.exp(jax.random.uniform(jax.random.fold_in(own, dim), (blocks,), jnp.float32, smallest / len(cuts), high / len(cuts)))
        level = level * jnp.repeat(draws, dims[dim] // blocks).reshape([-1 if axis == dim else 1 for axis in range(len(dims))])
    return level


def scatter_about(key, shape, width, bound, cuts=(), held_as=jnp.bfloat16):
    result = width * jax.random.normal(key, shape, jnp.float32)
    if cuts:
        result = result * level_of(key, shape, cuts, -0.22, 0.18)
    return jnp.clip(result, -bound, bound).astype(held_as)


def setup_inputs(seed: int = 0) -> dict:
    splits = jax.random.split(jax.random.key(seed), 8)
    queries = draw_queries(jax.random.fold_in(splits[7], 71), 0)
    keys = draw_keys(jax.random.fold_in(splits[7], 71), 0)
    values = scatter_about(splits[2], (TOTAL_TOKENS, KEY_VALUE_HEADS * HEAD_WIDTH), 1.0, 6.0, ((0, 256),))
    grad_out = scatter_about(splits[3], (TOTAL_TOKENS, QUERY_HEAD_COUNT * HEAD_WIDTH), 2.0, 12.0, ((0, 256),))
    chosen_len = touch_ends(jax.random.randint(splits[4], (PAIRS,), PAIR_TOKENS // 16, PAIR_TOKENS - PAIR_TOKENS // 16 + 1), jax.random.fold_in(splits[4], 1), PAIR_TOKENS // 16, (PAIR_TOKENS - PAIR_TOKENS // 16 + 1) - 1).astype(jnp.int32)
    pack_of = draw_pack_of(jax.random.fold_in(splits[7], 71), 0)
    pack_offset = draw_pack_offset(jax.random.fold_in(splits[7], 71), 0)
    return dict(queries=queries, keys=keys, values=values, grad_out=grad_out, chosen_len=chosen_len, pack_of=pack_of, pack_offset=pack_offset)


def round_half(array):
    return lax.optimization_barrier(array.astype(jnp.bfloat16)).astype(jnp.float32)

def pair_grads(query_row_block, key_row_block, value_row_block, gradient_rows, chosen):
    scale = 1.0 / math.sqrt(HEAD_WIDTH)
    position = jnp.arange(PAIR_TOKENS, dtype=jnp.int32)
    segment = (position >= chosen).astype(jnp.int32)
    allowed = (segment[:, None] == segment[None, :]) & (position[None, :] <= position[:, None])
    query_four = query_row_block.astype(jnp.float32).reshape(PAIR_TOKENS, KEY_VALUE_HEADS, QUERY_PER_KEY, HEAD_WIDTH)
    key_three = key_row_block.astype(jnp.float32).reshape(PAIR_TOKENS, KEY_VALUE_HEADS, HEAD_WIDTH)
    value_three = value_row_block.astype(jnp.float32).reshape(PAIR_TOKENS, KEY_VALUE_HEADS, HEAD_WIDTH)
    gradient_four = gradient_rows.astype(jnp.float32).reshape(PAIR_TOKENS, KEY_VALUE_HEADS, QUERY_PER_KEY, HEAD_WIDTH)
    scores = jnp.einsum('rhgd,shd->hgrs', query_four, key_three) * scale
    scores = jnp.where(allowed[None, None], scores, -jnp.inf)
    peak = lax.optimization_barrier(jnp.max(scores, axis=-1, keepdims=True))
    weights = jnp.exp(scores - peak)
    probs = weights / lax.optimization_barrier(jnp.sum(weights, axis=-1, keepdims=True))
    probs_b = round_half(probs)
    attended = jnp.einsum('hgrs,shd->rhgd', probs_b, value_three)
    delta = lax.optimization_barrier(jnp.sum(gradient_four * attended, axis=-1))
    dprob = jnp.einsum('rhgd,shd->hgrs', gradient_four, value_three)
    dscore = probs * (dprob - jnp.transpose(delta, (1, 2, 0))[..., None])
    dscore_b = round_half(dscore)
    pair_query_gradient = jnp.einsum('hgrs,shd->rhgd', dscore_b, key_three) * scale
    pair_key_gradient = jnp.einsum('hgrs,rhgd->shd', dscore_b, query_four) * scale
    pair_value_gradient = jnp.einsum('hgrs,rhgd->shd', probs_b, gradient_four)
    return (pair_query_gradient.reshape(PAIR_TOKENS, QUERY_HEAD_COUNT * HEAD_WIDTH).astype(jnp.bfloat16), pair_key_gradient.reshape(PAIR_TOKENS, KEY_VALUE_HEADS * HEAD_WIDTH).astype(jnp.bfloat16), pair_value_gradient.reshape(PAIR_TOKENS, KEY_VALUE_HEADS * HEAD_WIDTH).astype(jnp.bfloat16))

def reference(queries, keys, values, grad_out, chosen_len, pack_of, pack_offset):
    dest_block = (pack_of * (PACK // PAIR_TOKENS) + pack_offset // PAIR_TOKENS).astype(jnp.int32)
    source = jnp.zeros((PAIRS,), jnp.int32).at[dest_block].set(jnp.arange(PAIRS, dtype=jnp.int32))

    def single(index):
        start = (index * PAIR_TOKENS).astype(jnp.int32)
        query_row_block = lax.dynamic_slice_in_dim(queries, start, PAIR_TOKENS, 0)
        key_row_block = lax.dynamic_slice_in_dim(keys, start, PAIR_TOKENS, 0)
        value_row_block = lax.dynamic_slice_in_dim(values, start, PAIR_TOKENS, 0)
        gradient_rows = lax.dynamic_slice_in_dim(grad_out, start, PAIR_TOKENS, 0)
        return pair_grads(query_row_block, key_row_block, value_row_block, gradient_rows, chosen_len[index])
    query_gradient, key_gradient, value_gradient = lax.map(single, source)
    return (query_gradient.reshape(TOTAL_TOKENS, QUERY_HEAD_COUNT * HEAD_WIDTH), key_gradient.reshape(TOTAL_TOKENS, KEY_VALUE_HEADS * HEAD_WIDTH), value_gradient.reshape(TOTAL_TOKENS, KEY_VALUE_HEADS * HEAD_WIDTH))
```

```python
import functools
import math

import jax
import jax.numpy as jnp
from jax import lax
from jax.experimental import pallas as pl
from jax.experimental.pallas import tpu as pltpu
from jax.sharding import PartitionSpec as P

WIDTH = 128
PAIR = 256
HALF = 128
GROUP = 4
BOTH = ("dp", "tensor")
CONTRACT_LAST = (((1,), (1,)), ((), ()))
CONTRACT_FIRST = (((0,), (0,)), ((), ()))


def attention_kernel(info, q_ref, g_ref, k_ref, v_ref, kp_ref, vp_ref, x_ref, own_ref, part_ref):
    chosen = info[0]
    second = info[1]
    scale = 1.0 / math.sqrt(WIDTH)
    f32 = jnp.float32
    bf16 = jnp.bfloat16

    row = lax.broadcasted_iota(jnp.int32, (HALF, PAIR), 0) + HALF * second
    col = lax.broadcasted_iota(jnp.int32, (HALF, PAIR), 1) - HALF * (1 - second)
    low = jnp.where(row >= chosen, chosen, 0)
    allowed = (col >= low) & (col <= row)

    q4 = jnp.concatenate([q_ref[:, i * WIDTH : (i + 1) * WIDTH] for i in range(GROUP)], axis=0)
    g4 = jnp.concatenate([g_ref[:, i * WIDTH : (i + 1) * WIDTH] for i in range(GROUP)], axis=0)
    kc = jnp.concatenate([kp_ref[...], k_ref[...]], axis=0)
    vc = jnp.concatenate([vp_ref[...], v_ref[...]], axis=0)

    scores = lax.dot_general(q4, kc, CONTRACT_LAST, preferred_element_type=f32) * scale
    dprob = lax.dot_general(g4, vc, CONTRACT_LAST, preferred_element_type=f32)
    scores = jnp.where(allowed[None], scores.reshape(GROUP, HALF, PAIR), -1e30).reshape(GROUP * HALF, PAIR)
    peak = jnp.max(scores, axis=1, keepdims=True)
    weights = jnp.exp(scores - peak)
    probs = weights * (1.0 / jnp.sum(weights, axis=1, keepdims=True))
    probs_b = probs.astype(bf16)
    delta = jnp.sum(probs_b.astype(f32) * dprob, axis=1, keepdims=True)
    dscore_b = (probs * (dprob - delta)).astype(bf16)
    dq = lax.dot_general(dscore_b, kc, (((1,), (0,)), ((), ())), preferred_element_type=f32) * scale
    dk = lax.dot_general(dscore_b, q4, CONTRACT_FIRST, preferred_element_type=f32) * scale
    dv = lax.dot_general(probs_b, g4, CONTRACT_FIRST, preferred_element_type=f32)

    def tiles(block):
        return block.reshape(HALF // 8, 8, WIDTH)

    for i in range(GROUP):
        x_ref[:, i // 2, :, (i % 2) * WIDTH : (i % 2 + 1) * WIDTH] = tiles(dq[i * HALF : (i + 1) * HALF]).astype(bf16)
    own_ref[:, 0] = tiles(dk[HALF:])
    own_ref[:, 1] = tiles(dv[HALF:])
    part_ref[:, 0] = tiles(dk[:HALF]).astype(bf16)
    part_ref[:, 1] = tiles(dv[:HALF]).astype(bf16)


def attention(info, q, g, k, v, kp, vp):
    heads = k.shape[1] // WIDTH
    groups = HALF // 8
    narrow = pl.BlockSpec((HALF, WIDTH), lambda h, info: (0, h))
    wide = pl.BlockSpec((HALF, GROUP * WIDTH), lambda h, info: (0, h))
    small = pl.BlockSpec((groups, 2, 8, WIDTH), lambda h, info: (0, h, 0, 0))
    return pl.pallas_call(
        attention_kernel,
        grid_spec=pltpu.PrefetchScalarGridSpec(
            num_scalar_prefetch=1,
            grid=(heads,),
            in_specs=[wide, wide, narrow, narrow, narrow, narrow],
            out_specs=[pl.BlockSpec((groups, 2, 8, 3 * WIDTH), lambda h, info: (0, h, 0, 0)), small, small],
        ),
        out_shape=[
            jax.ShapeDtypeStruct((groups, 2 * heads, 8, 3 * WIDTH), jnp.bfloat16),
            jax.ShapeDtypeStruct((groups, 2 * heads, 8, WIDTH), jnp.float32),
            jax.ShapeDtypeStruct((groups, 2 * heads, 8, WIDTH), jnp.bfloat16),
        ],
        compiler_params=pltpu.CompilerParams(vmem_limit_bytes=32 * 1024 * 1024),
        name="attention",
    )(info, q, g, k, v, kp, vp)


def combine_kernel(own_ref, part_ref, x_in, x_ref):
    del x_in
    x_ref[...] = (own_ref[...] + part_ref[...].astype(jnp.float32)).astype(jnp.bfloat16)


def combine(own, part, x):
    whole = pl.BlockSpec(own.shape, lambda i: (0, 0, 0, 0))
    return pl.pallas_call(
        combine_kernel,
        grid=(1,),
        in_specs=[whole, whole, pl.BlockSpec(memory_space=pl.ANY)],
        out_specs=pl.BlockSpec(own.shape, lambda i: (0, 0, 0, 2)),
        out_shape=jax.ShapeDtypeStruct(x.shape, x.dtype),
        input_output_aliases={2: 0},
        compiler_params=pltpu.CompilerParams(vmem_limit_bytes=32 * 1024 * 1024),
        name="combine",
    )(own, part, x)


def reorder_kernel(pack_of, pack_offset, y_ref, x_ref, sem):
    pairs = y_ref.shape[0]

    def step(i, carry):
        block = pack_of[i] * (1024 // PAIR) + pack_offset[i] // PAIR
        pltpu.make_async_copy(y_ref.at[i], x_ref.at[block], sem).start()
        return carry

    lax.fori_loop(0, pairs, step, 0)
    pltpu.make_async_copy(y_ref, x_ref, sem).wait()


def reorder(pack_of, pack_offset, y):
    return pl.pallas_call(
        reorder_kernel,
        grid_spec=pltpu.PrefetchScalarGridSpec(
            num_scalar_prefetch=2,
            grid=(1,),
            in_specs=[pl.BlockSpec(memory_space=pl.ANY)],
            out_specs=pl.BlockSpec(memory_space=pl.ANY),
            scratch_shapes=[pltpu.SemaphoreType.DMA],
        ),
        out_shape=jax.ShapeDtypeStruct(y.shape, y.dtype),
        name="reorder",
    )(pack_of, pack_offset, y)


def place_kernel(z_ref, q_ref, k_ref, v_ref):
    def rows(block):
        return block.astype(jnp.float32).reshape(HALF, block.shape[-1]).astype(jnp.bfloat16)

    q_ref[:, : 2 * WIDTH] = rows(z_ref[:, 0, :, : 2 * WIDTH])
    q_ref[:, 2 * WIDTH :] = rows(z_ref[:, 1, :, : 2 * WIDTH])
    k_ref[...] = rows(z_ref[:, 0, :, 2 * WIDTH :])
    v_ref[...] = rows(z_ref[:, 1, :, 2 * WIDTH :])


def place(z):
    groups, double, _, _ = z.shape
    heads = double // 2
    narrow = pl.BlockSpec((HALF, WIDTH), lambda h: (0, h))
    return pl.pallas_call(
        place_kernel,
        grid=(heads,),
        in_specs=[pl.BlockSpec((groups, 2, 8, 3 * WIDTH), lambda h: (0, h, 0, 0))],
        out_specs=[pl.BlockSpec((HALF, GROUP * WIDTH), lambda h: (0, h)), narrow, narrow],
        out_shape=[
            jax.ShapeDtypeStruct((HALF, heads * GROUP * WIDTH), jnp.bfloat16),
            jax.ShapeDtypeStruct((HALF, heads * WIDTH), jnp.bfloat16),
            jax.ShapeDtypeStruct((HALF, heads * WIDTH), jnp.bfloat16),
        ],
        compiler_params=pltpu.CompilerParams(vmem_limit_bytes=32 * 1024 * 1024),
        name="place",
    )(z)


def per_device(queries, keys, values, grad_out, chosen_len, pack_of, pack_offset):
    tensor_count = lax.axis_size("tensor")
    devices = tensor_count * lax.axis_size("dp")
    tensor_here = lax.axis_index("tensor")
    device_here = lax.axis_index("dp") * tensor_count + tensor_here
    info = jnp.stack([chosen_len[device_here // 2], tensor_here % 2]).astype(jnp.int32)

    up = [(i, i + 1) for i in range(0, tensor_count, 2)]
    down = [(i + 1, i) for i in range(0, tensor_count, 2)]
    first_keys = lax.ppermute(keys, "tensor", up)
    first_values = lax.ppermute(values, "tensor", up)
    pieces, own, part = attention(info, queries, grad_out, keys, values, first_keys, first_values)
    part = lax.ppermute(part, "tensor", down)
    pieces = combine(own, part, pieces)
    shape = pieces.shape
    spread = lax.all_to_all(pieces.reshape(devices, 8, 3 * WIDTH), BOTH, split_axis=0, concat_axis=0, tiled=True)
    ordered = reorder(pack_of, pack_offset, spread.reshape(devices // 2, 2, 8, 3 * WIDTH))
    gathered = lax.all_to_all(ordered.reshape(devices, 8, 3 * WIDTH), BOTH, split_axis=0, concat_axis=0, tiled=True)
    return tuple(place(gathered.reshape(shape)))


def solution(mesh):
    rows = P(BOTH, None)
    return jax.shard_map(
        per_device,
        mesh=mesh,
        in_specs=(rows, rows, rows, rows, P(), P(), P()),
        out_specs=(rows, rows, rows),
        check_vma=False,
    )
```

```python
import functools
import math

import jax
import jax.numpy as jnp
from jax import lax
from jax.experimental import pallas as pl
from jax.experimental.pallas import tpu as pltpu
from jax.sharding import PartitionSpec as P

WIDTH = 128
PAIR = 256
HALF = 128
GROUP = 4
CHUNKS = 2
VMEM_ATT = 32
BOTH = ("dp", "tensor")
CONTRACT_LAST = (((1,), (1,)), ((), ()))
CONTRACT_FIRST = (((0,), (0,)), ((), ()))


def attention_kernel(info, q_ref, g_ref, k_ref, v_ref, kp_ref, vp_ref, x_ref, own_ref, part_ref):
    chosen = info[0]
    second = info[1]
    scale = 1.0 / math.sqrt(WIDTH)
    f32 = jnp.float32
    bf16 = jnp.bfloat16

    row = lax.broadcasted_iota(jnp.int32, (HALF, PAIR), 0) + HALF * second
    col = lax.broadcasted_iota(jnp.int32, (HALF, PAIR), 1) - HALF * (1 - second)
    low = jnp.where(row >= chosen, chosen, 0)
    allowed = (col >= low) & (col <= row)

    q4 = jnp.concatenate([q_ref[:, i * WIDTH : (i + 1) * WIDTH] for i in range(GROUP)], axis=0)
    g4 = jnp.concatenate([g_ref[:, i * WIDTH : (i + 1) * WIDTH] for i in range(GROUP)], axis=0)
    kc = jnp.concatenate([kp_ref[...], k_ref[...]], axis=0)
    vc = jnp.concatenate([vp_ref[...], v_ref[...]], axis=0)

    scores = lax.dot_general(q4, kc, CONTRACT_LAST, preferred_element_type=f32) * scale
    dprob = lax.dot_general(g4, vc, CONTRACT_LAST, preferred_element_type=f32)
    scores = jnp.where(allowed[None], scores.reshape(GROUP, HALF, PAIR), -1e30).reshape(GROUP * HALF, PAIR)
    peak = jnp.max(scores, axis=1, keepdims=True)
    weights = jnp.exp(scores - peak)
    probs = weights * (1.0 / jnp.sum(weights, axis=1, keepdims=True))
    probs_b = probs.astype(bf16)
    delta = jnp.sum(probs_b.astype(f32) * dprob, axis=1, keepdims=True)
    dscore_b = (probs * (dprob - delta)).astype(bf16)
    dq = lax.dot_general(dscore_b, kc, (((1,), (0,)), ((), ())), preferred_element_type=f32) * scale
    dk = lax.dot_general(dscore_b, q4, CONTRACT_FIRST, preferred_element_type=f32) * scale
    dv = lax.dot_general(probs_b, g4, CONTRACT_FIRST, preferred_element_type=f32)

    def tiles(block):
        return block.reshape(HALF // 8, 8, WIDTH)

    for i in range(GROUP):
        x_ref[:, i // 2, :, (i % 2) * WIDTH : (i % 2 + 1) * WIDTH] = tiles(dq[i * HALF : (i + 1) * HALF]).astype(bf16)
    own_ref[:, 0] = tiles(dk[HALF:])
    own_ref[:, 1] = tiles(dv[HALF:])
    part_ref[:, 0] = tiles(dk[:HALF]).astype(bf16)
    part_ref[:, 1] = tiles(dv[:HALF]).astype(bf16)


def attention(info, q, g, k, v, first, chunk, chunks, x=None):
    all_heads = k.shape[1] // WIDTH
    heads = all_heads // chunks
    base = chunk * heads
    groups = HALF // 8
    narrow = pl.BlockSpec((HALF, WIDTH), lambda h, info: (0, base + h))
    wide = pl.BlockSpec((HALF, GROUP * WIDTH), lambda h, info: (0, base + h))
    first_key = pl.BlockSpec((HALF, WIDTH), lambda h, info: (0, h))
    first_value = pl.BlockSpec((HALF, WIDTH), lambda h, info: (0, heads + h))
    small = pl.BlockSpec((groups, 2, 8, WIDTH), lambda h, info: (0, h, 0, 0))
    shared = [] if x is None else [x]

    def body(info, *refs):
        attention_kernel(info, *refs[:6], *refs[6 + len(shared) :])

    return pl.pallas_call(
        body,
        grid_spec=pltpu.PrefetchScalarGridSpec(
            num_scalar_prefetch=1,
            grid=(heads,),
            in_specs=[wide, wide, narrow, narrow, first_key, first_value]
            + [pl.BlockSpec(memory_space=pl.ANY)] * len(shared),
            out_specs=[pl.BlockSpec((groups, 2, 8, 3 * WIDTH), lambda h, info: (0, base + h, 0, 0)), small, small],
        ),
        out_shape=[
            jax.ShapeDtypeStruct((groups, 2 * all_heads, 8, 3 * WIDTH), jnp.bfloat16),
            jax.ShapeDtypeStruct((groups, 2 * heads, 8, WIDTH), jnp.float32),
            jax.ShapeDtypeStruct((groups, 2 * heads, 8, WIDTH), jnp.bfloat16),
        ],
        input_output_aliases={7: 0} if shared else {},
        compiler_params=pltpu.CompilerParams(vmem_limit_bytes=VMEM_ATT * 1024 * 1024),
        name=f"attention{chunk}",
    )(info, q, g, k, v, first, first, *shared)


def combine_kernel(*refs):
    chunks = (len(refs) - 2) // 2
    x_ref = refs[-1]
    for c in range(chunks):
        own_ref, part_ref = refs[2 * c], refs[2 * c + 1]
        size = own_ref.shape[1]
        total = own_ref[...] + part_ref[...].astype(jnp.float32)
        x_ref[:, c * size : (c + 1) * size] = total.astype(jnp.bfloat16)


def combine(owns, parts, x):
    shape = x.shape[:3] + (WIDTH,)
    operands = [a for pair in zip(owns, parts) for a in pair]
    return pl.pallas_call(
        combine_kernel,
        grid=(1,),
        in_specs=[pl.BlockSpec(a.shape, lambda i: (0, 0, 0, 0)) for a in operands] + [pl.BlockSpec(memory_space=pl.ANY)],
        out_specs=pl.BlockSpec(shape, lambda i: (0, 0, 0, 2)),
        out_shape=jax.ShapeDtypeStruct(x.shape, x.dtype),
        input_output_aliases={len(operands): 0},
        compiler_params=pltpu.CompilerParams(vmem_limit_bytes=16 * 1024 * 1024),
        name="combine",
    )(*operands, x)


def reorder_kernel(pack_of, pack_offset, y_ref, x_ref):
    def step(i, carry):
        block = pack_of[i] * (1024 // PAIR) + pack_offset[i] // PAIR
        x_ref[block] = y_ref[i]
        return carry

    lax.fori_loop(0, y_ref.shape[0], step, 0, unroll=8)


def reorder(pack_of, pack_offset, y):
    whole = pl.BlockSpec(y.shape, lambda i, *_: (0,) * y.ndim)
    return pl.pallas_call(
        reorder_kernel,
        grid_spec=pltpu.PrefetchScalarGridSpec(
            num_scalar_prefetch=2, grid=(1,), in_specs=[whole], out_specs=whole
        ),
        out_shape=jax.ShapeDtypeStruct(y.shape, y.dtype),
        compiler_params=pltpu.CompilerParams(vmem_limit_bytes=16 * 1024 * 1024),
        name="reorder",
    )(pack_of, pack_offset, y)


def place_kernel(z_ref, q_ref, k_ref, v_ref):
    def rows(block):
        return block.astype(jnp.float32).reshape(HALF, block.shape[-1]).astype(jnp.bfloat16)

    q_ref[:, : 2 * WIDTH] = rows(z_ref[:, 0, :, : 2 * WIDTH])
    q_ref[:, 2 * WIDTH :] = rows(z_ref[:, 1, :, : 2 * WIDTH])
    k_ref[...] = rows(z_ref[:, 0, :, 2 * WIDTH :])
    v_ref[...] = rows(z_ref[:, 1, :, 2 * WIDTH :])


def place(z):
    groups, double, _, _ = z.shape
    heads = double // 2
    narrow = pl.BlockSpec((HALF, WIDTH), lambda h: (0, h))
    return pl.pallas_call(
        place_kernel,
        grid=(heads,),
        in_specs=[pl.BlockSpec((groups, 2, 8, 3 * WIDTH), lambda h: (0, h, 0, 0))],
        out_specs=[pl.BlockSpec((HALF, GROUP * WIDTH), lambda h: (0, h)), narrow, narrow],
        out_shape=[
            jax.ShapeDtypeStruct((HALF, heads * GROUP * WIDTH), jnp.bfloat16),
            jax.ShapeDtypeStruct((HALF, heads * WIDTH), jnp.bfloat16),
            jax.ShapeDtypeStruct((HALF, heads * WIDTH), jnp.bfloat16),
        ],
        compiler_params=pltpu.CompilerParams(vmem_limit_bytes=32 * 1024 * 1024),
        name="place",
    )(z)


def per_device(queries, keys, values, grad_out, chosen_len, pack_of, pack_offset):
    tensor_count = lax.axis_size("tensor")
    devices = tensor_count * lax.axis_size("dp")
    tensor_here = lax.axis_index("tensor")
    device_here = lax.axis_index("dp") * tensor_count + tensor_here
    info = jnp.stack([chosen_len[device_here // 2], tensor_here % 2]).astype(jnp.int32)

    up = [(i, i + 1) for i in range(0, tensor_count, 2)]
    down = [(i + 1, i) for i in range(0, tensor_count, 2)]
    span = keys.shape[1] // CHUNKS
    cuts = [slice(c * span, (c + 1) * span) for c in range(CHUNKS)]
    firsts = [lax.ppermute(jnp.concatenate([keys[:, cut], values[:, cut]], axis=1), "tensor", up) for cut in cuts]
    pieces, owns, parts = None, [], []
    for c in range(CHUNKS):
        pieces, own, part = attention(info, queries, grad_out, keys, values, firsts[c], c, CHUNKS, pieces)
        owns.append(own)
        parts.append(lax.ppermute(part, "tensor", down))
    pieces = combine(owns, parts, pieces)
    shape = pieces.shape
    spread = lax.all_to_all(pieces.reshape(devices, 8, 3 * WIDTH), BOTH, split_axis=0, concat_axis=0, tiled=True)
    ordered = reorder(pack_of, pack_offset, spread.reshape(devices // 2, 2, 8, 3 * WIDTH))
    gathered = lax.all_to_all(ordered.reshape(devices, 8, 3 * WIDTH), BOTH, split_axis=0, concat_axis=0, tiled=True)
    return tuple(place(gathered.reshape(shape)))


def solution(mesh):
    rows = P(BOTH, None)
    return jax.shard_map(
        per_device,
        mesh=mesh,
        in_specs=(rows, rows, rows, rows, P(), P(), P()),
        out_specs=(rows, rows, rows),
        check_vma=False,
    )
```

```python
import functools
import math

import jax
import jax.numpy as jnp
from jax import lax
from jax.experimental import pallas as pl
from jax.experimental.pallas import tpu as pltpu
from jax.sharding import PartitionSpec as P

WIDTH = 128
PAIR = 256
HALF = 128
GROUP = 4
CHUNKS = (4, 4)
VMEM_ATT = 32
PLACE_STEPS = 2
BOTH = ("dp", "tensor")
CONTRACT_LAST = (((1,), (1,)), ((), ()))
CONTRACT_FIRST = (((0,), (0,)), ((), ()))


def attention_kernel(lo, hi, info, q_ref, g_ref, own_ref, first_ref, dq_ref, mine_ref, part_ref):
    chosen = info[0]
    second = info[1]
    scale = 1.0 / math.sqrt(WIDTH)
    f32 = jnp.float32
    bf16 = jnp.bfloat16
    heads = hi - lo

    row = lax.broadcasted_iota(jnp.int32, (HALF, PAIR), 0) + HALF * second
    col = lax.broadcasted_iota(jnp.int32, (HALF, PAIR), 1) - HALF * (1 - second)
    low = jnp.where(row >= chosen, chosen, 0)
    allowed = (col >= low) & (col <= row)

    def four(ref, h):
        left = (lo + h) * GROUP * WIDTH
        return jnp.concatenate([ref[:, left + i * WIDTH : left + (i + 1) * WIDTH] for i in range(GROUP)], axis=0)

    def both(h):
        at = slice(h * WIDTH, (h + 1) * WIDTH)
        return jnp.concatenate([first_ref[:, at], own_ref[:, at]], axis=0)

    def tiles(block):
        return block.reshape(HALF // 8, 8, WIDTH)

    products = []
    for h in range(heads):
        scores = lax.dot_general(four(q_ref, h), both(h), CONTRACT_LAST, preferred_element_type=f32)
        dprob = lax.dot_general(four(g_ref, h), both(heads + h), CONTRACT_LAST, preferred_element_type=f32)
        products.append((scores, dprob))
    factors = []
    for scores, dprob in products:
        scores = jnp.where(allowed[None], scores.reshape(GROUP, HALF, PAIR), -1e30).reshape(GROUP * HALF, PAIR)
        peak = jnp.max(scores, axis=1, keepdims=True)
        weights = jnp.exp2((scores - peak) * (scale * math.log2(math.e)))
        probs = weights * (1.0 / jnp.sum(weights, axis=1, keepdims=True))
        probs_b = probs.astype(bf16)
        delta = jnp.sum(probs_b.astype(f32) * dprob, axis=1, keepdims=True)
        factors.append((probs_b, (probs * (dprob - delta)).astype(bf16)))
    for h, (probs_b, dscore_b) in enumerate(factors):
        dq = jnp.dot(dscore_b, both(h), preferred_element_type=f32) * scale
        dk = lax.dot_general(dscore_b, four(q_ref, h), CONTRACT_FIRST, preferred_element_type=f32) * scale
        dv = lax.dot_general(probs_b, four(g_ref, h), CONTRACT_FIRST, preferred_element_type=f32)
        for i in range(GROUP):
            at = slice((i % 2) * WIDTH, (i % 2 + 1) * WIDTH)
            dq_ref[:, 2 * h + i // 2, :, at] = tiles(dq[i * HALF : (i + 1) * HALF]).astype(bf16)
        mine_ref[:, 2 * h] = tiles(dk[HALF:])
        mine_ref[:, 2 * h + 1] = tiles(dv[HALF:])
        part_ref[:, 2 * h] = tiles(dk[:HALF]).astype(bf16)
        part_ref[:, 2 * h + 1] = tiles(dv[:HALF]).astype(bf16)


def whole(shape):
    return pl.BlockSpec(shape, lambda i, *_: (0,) * len(shape))


def attention(info, q, g, own, first, lo, hi):
    rows = (HALF // 8, 2 * (hi - lo), 8)
    outs = [
        jax.ShapeDtypeStruct(rows + (2 * WIDTH,), jnp.bfloat16),
        jax.ShapeDtypeStruct(rows + (WIDTH,), jnp.float32),
        jax.ShapeDtypeStruct(rows + (WIDTH,), jnp.bfloat16),
    ]
    return pl.pallas_call(
        functools.partial(attention_kernel, lo, hi),
        grid_spec=pltpu.PrefetchScalarGridSpec(
            num_scalar_prefetch=1,
            grid=(1,),
            in_specs=[whole(a.shape) for a in (q, g, own, first)],
            out_specs=[whole(a.shape) for a in outs],
        ),
        out_shape=outs,
        compiler_params=pltpu.CompilerParams(vmem_limit_bytes=VMEM_ATT * 1024 * 1024),
        name=f"attention{lo}",
    )(info, q, g, own, first)


def combine_kernel(*refs):
    x_ref = refs[-1]
    at = 0
    for c in range(len(refs) // 3):
        dq_ref, mine_ref, part_ref = refs[3 * c : 3 * c + 3]
        size = dq_ref.shape[1]
        total = mine_ref[...] + part_ref[...].astype(jnp.float32)
        x_ref[:, at : at + size, :, : 2 * WIDTH] = dq_ref[...]
        x_ref[:, at : at + size, :, 2 * WIDTH :] = total.astype(jnp.bfloat16)
        at += size


def combine(parts, heads):
    shape = (HALF // 8, 2 * heads, 8, 3 * WIDTH)
    operands = [a for part in parts for a in part]
    return pl.pallas_call(
        combine_kernel,
        grid=(1,),
        in_specs=[whole(a.shape) for a in operands],
        out_specs=whole(shape),
        out_shape=jax.ShapeDtypeStruct(shape, jnp.bfloat16),
        compiler_params=pltpu.CompilerParams(vmem_limit_bytes=16 * 1024 * 1024),
        name="combine",
    )(*operands)


def reorder_kernel(pack_of, pack_offset, y_ref, x_ref):
    def step(i, carry):
        block = pack_of[i] * (1024 // PAIR) + pack_offset[i] // PAIR
        x_ref[block] = y_ref[i]
        return carry

    lax.fori_loop(0, y_ref.shape[0], step, 0, unroll=8)


def reorder(pack_of, pack_offset, y):
    return pl.pallas_call(
        reorder_kernel,
        grid_spec=pltpu.PrefetchScalarGridSpec(
            num_scalar_prefetch=2, grid=(1,), in_specs=[whole(y.shape)], out_specs=whole(y.shape)
        ),
        out_shape=jax.ShapeDtypeStruct(y.shape, y.dtype),
        compiler_params=pltpu.CompilerParams(vmem_limit_bytes=16 * 1024 * 1024),
        name="reorder",
    )(pack_of, pack_offset, y)


def place_kernel(z_ref, q_ref, k_ref, v_ref):
    def rows(block):
        return block.astype(jnp.float32).reshape(HALF, block.shape[-1]).astype(jnp.bfloat16)

    for h in range(z_ref.shape[1] // 2):
        left = h * GROUP * WIDTH
        q_ref[:, left : left + 2 * WIDTH] = rows(z_ref[:, 2 * h, :, : 2 * WIDTH])
        q_ref[:, left + 2 * WIDTH : left + 4 * WIDTH] = rows(z_ref[:, 2 * h + 1, :, : 2 * WIDTH])
        k_ref[:, h * WIDTH : (h + 1) * WIDTH] = rows(z_ref[:, 2 * h, :, 2 * WIDTH :])
        v_ref[:, h * WIDTH : (h + 1) * WIDTH] = rows(z_ref[:, 2 * h + 1, :, 2 * WIDTH :])


def place(z):
    groups, double, _, _ = z.shape
    heads = double // 2
    step = heads // PLACE_STEPS
    narrow = pl.BlockSpec((HALF, step * WIDTH), lambda h: (0, h))
    return pl.pallas_call(
        place_kernel,
        grid=(PLACE_STEPS,),
        in_specs=[pl.BlockSpec((groups, 2 * step, 8, 3 * WIDTH), lambda h: (0, h, 0, 0))],
        out_specs=[pl.BlockSpec((HALF, step * GROUP * WIDTH), lambda h: (0, h)), narrow, narrow],
        out_shape=[
            jax.ShapeDtypeStruct((HALF, heads * GROUP * WIDTH), jnp.bfloat16),
            jax.ShapeDtypeStruct((HALF, heads * WIDTH), jnp.bfloat16),
            jax.ShapeDtypeStruct((HALF, heads * WIDTH), jnp.bfloat16),
        ],
        compiler_params=pltpu.CompilerParams(vmem_limit_bytes=32 * 1024 * 1024),
        name="place",
    )(z)


def per_device(queries, keys, values, grad_out, chosen_len, pack_of, pack_offset):
    tensor_count = lax.axis_size("tensor")
    devices = tensor_count * lax.axis_size("dp")
    tensor_here = lax.axis_index("tensor")
    device_here = lax.axis_index("dp") * tensor_count + tensor_here
    info = jnp.stack([chosen_len[device_here // 2], tensor_here % 2]).astype(jnp.int32)

    up = [(i, i + 1) for i in range(0, tensor_count, 2)]
    down = [(i + 1, i) for i in range(0, tensor_count, 2)]
    heads = keys.shape[1] // WIDTH
    bounds = [0]
    for share in CHUNKS:
        bounds.append(bounds[-1] + share * heads // sum(CHUNKS))
    cuts = list(zip(bounds[:-1], bounds[1:]))
    owns = [
        jnp.concatenate([keys[:, lo * WIDTH : hi * WIDTH], values[:, lo * WIDTH : hi * WIDTH]], axis=1)
        for lo, hi in cuts
    ]
    firsts = [lax.ppermute(own, "tensor", up) for own in owns]
    parts = []
    for (lo, hi), own, first in zip(cuts, owns, firsts):
        dq, mine, part = attention(info, queries, grad_out, own, first, lo, hi)
        parts.append((dq, mine, lax.ppermute(part, "tensor", down)))
    pieces = combine(parts, heads)
    shape = pieces.shape
    spread = lax.all_to_all(pieces.reshape(devices, 8, 3 * WIDTH), BOTH, split_axis=0, concat_axis=0, tiled=True)
    ordered = reorder(pack_of, pack_offset, spread.reshape(devices // 2, 2, 8, 3 * WIDTH))
    gathered = lax.all_to_all(ordered.reshape(devices, 8, 3 * WIDTH), BOTH, split_axis=0, concat_axis=0, tiled=True)
    return tuple(place(gathered.reshape(shape)))


def solution(mesh):
    rows = P(BOTH, None)
    return jax.shard_map(
        per_device,
        mesh=mesh,
        in_specs=(rows, rows, rows, rows, P(), P(), P()),
        out_specs=(rows, rows, rows),
        check_vma=False,
    )
```

```python
import functools
import math

import jax
import jax.numpy as jnp
from jax import lax
from jax.experimental import pallas as pl
from jax.experimental.pallas import tpu as pltpu
from jax.sharding import PartitionSpec as P

WIDTH = 128
PAIR = 256
HALF = 128
GROUP = 4
CHUNKS = (4, 4)
VMEM_ATT = 32
PLACE_STEPS = 2
TILE = 16
PAIRS_OVER = ("dp", "slot")
ALL = ("dp", "slot", "half")
CONTRACT_LAST = (((1,), (1,)), ((), ()))
CONTRACT_FIRST = (((0,), (0,)), ((), ()))


def attention_kernel(lo, hi, info_ref, q_ref, g_ref, own_ref, first_ref, dq_ref, mine_ref, part_ref):
    chosen = info_ref[0:1, :]
    second = info_ref[8:9, :]
    scale = 1.0 / math.sqrt(WIDTH)
    f32 = jnp.float32
    bf16 = jnp.bfloat16
    heads = hi - lo

    row = lax.broadcasted_iota(jnp.int32, (HALF, PAIR), 0) + HALF * second
    col = lax.broadcasted_iota(jnp.int32, (HALF, PAIR), 1) - HALF * (1 - second)
    low = jnp.where(row >= chosen, chosen, 0)
    allowed = (col >= low) & (col <= row)

    def four(ref, h):
        left = (lo + h) * GROUP * WIDTH
        return jnp.concatenate([ref[:, left + i * WIDTH : left + (i + 1) * WIDTH] for i in range(GROUP)], axis=0)

    def both(h):
        at = slice(h * WIDTH, (h + 1) * WIDTH)
        return jnp.concatenate([first_ref[:, at], own_ref[:, at]], axis=0)

    def tiles(block):
        return block.reshape(HALF // TILE, TILE, WIDTH)

    products = []
    for h in range(heads):
        scores = lax.dot_general(four(q_ref, h), both(h), CONTRACT_LAST, preferred_element_type=f32)
        dprob = lax.dot_general(four(g_ref, h), both(heads + h), CONTRACT_LAST, preferred_element_type=f32)
        products.append((scores, dprob))
    factors = []
    for scores, dprob in products:
        scores = jnp.where(allowed[None], scores.reshape(GROUP, HALF, PAIR), -1e30).reshape(GROUP * HALF, PAIR)
        peak = jnp.max(scores, axis=1, keepdims=True)
        weights = jnp.exp2((scores - peak) * (scale * math.log2(math.e)))
        probs = weights * (1.0 / jnp.sum(weights, axis=1, keepdims=True))
        probs_b = probs.astype(bf16)
        delta = jnp.sum(probs_b.astype(f32) * dprob, axis=1, keepdims=True)
        factors.append((probs_b, (probs * (dprob - delta)).astype(bf16)))
    for h, (probs_b, dscore_b) in enumerate(factors):
        dq = jnp.dot(dscore_b, both(h), preferred_element_type=f32) * scale
        dk = lax.dot_general(dscore_b, four(q_ref, h), CONTRACT_FIRST, preferred_element_type=f32) * scale
        dv = lax.dot_general(probs_b, four(g_ref, h), CONTRACT_FIRST, preferred_element_type=f32)
        for i in range(GROUP):
            at = slice((i % 2) * WIDTH, (i % 2 + 1) * WIDTH)
            dq_ref[:, 2 * h + i // 2, :, at] = tiles(dq[i * HALF : (i + 1) * HALF]).astype(bf16)
        mine_ref[:, 2 * h] = tiles(dk[HALF:])
        mine_ref[:, 2 * h + 1] = tiles(dv[HALF:])
        part_ref[:, 2 * h] = tiles(dk[:HALF]).astype(bf16)
        part_ref[:, 2 * h + 1] = tiles(dv[:HALF]).astype(bf16)


def whole(shape):
    return pl.BlockSpec(shape, lambda i, *_: (0,) * len(shape))


def attention(info, q, g, own, first, lo, hi, before):
    rows = (HALF // TILE, 2 * (hi - lo), TILE)
    outs = [
        jax.ShapeDtypeStruct(rows + (2 * WIDTH,), jnp.bfloat16),
        jax.ShapeDtypeStruct(rows + (WIDTH,), jnp.float32),
        jax.ShapeDtypeStruct(rows + (WIDTH,), jnp.bfloat16),
    ]
    def body(*refs):
        attention_kernel(lo, hi, *refs[:5], *refs[5 + len(before) :])

    return pl.pallas_call(
        body,
        grid=(1,),
        in_specs=[whole(a.shape) for a in (info, q, g, own, first)] + [pl.BlockSpec(memory_space=pl.ANY)] * len(before),
        out_specs=[whole(a.shape) for a in outs],
        out_shape=outs,
        compiler_params=pltpu.CompilerParams(vmem_limit_bytes=VMEM_ATT * 1024 * 1024),
        name=f"attention{lo}",
    )(info, q, g, own, first, *before)


def combine_kernel(*refs):
    x_ref = refs[-1]
    at = 0
    for c in range(len(refs) // 3):
        dq_ref, mine_ref, part_ref = refs[3 * c : 3 * c + 3]
        size = dq_ref.shape[1]
        total = mine_ref[...] + part_ref[...].astype(jnp.float32)
        x_ref[:, at : at + size, :, : 2 * WIDTH] = dq_ref[...]
        x_ref[:, at : at + size, :, 2 * WIDTH :] = total.astype(jnp.bfloat16)
        at += size


def combine(parts, heads):
    shape = (HALF // TILE, 2 * heads, TILE, 3 * WIDTH)
    operands = [a for part in parts for a in part]
    return pl.pallas_call(
        combine_kernel,
        grid=(1,),
        in_specs=[whole(a.shape) for a in operands],
        out_specs=whole(shape),
        out_shape=jax.ShapeDtypeStruct(shape, jnp.bfloat16),
        compiler_params=pltpu.CompilerParams(vmem_limit_bytes=16 * 1024 * 1024),
        name="combine",
    )(*operands)


def reorder_kernel(pack_of, pack_offset, y_ref, x_ref):
    def step(i, carry):
        block = pack_of[i] * (1024 // PAIR) + pack_offset[i] // PAIR
        x_ref[block] = y_ref[i]
        return carry

    lax.fori_loop(0, y_ref.shape[0], step, 0, unroll=32)


def reorder(pack_of, pack_offset, y):
    return pl.pallas_call(
        reorder_kernel,
        grid_spec=pltpu.PrefetchScalarGridSpec(
            num_scalar_prefetch=2, grid=(1,), in_specs=[whole(y.shape)], out_specs=whole(y.shape)
        ),
        out_shape=jax.ShapeDtypeStruct(y.shape, y.dtype),
        compiler_params=pltpu.CompilerParams(vmem_limit_bytes=16 * 1024 * 1024),
        name="reorder",
    )(pack_of, pack_offset, y)


def place_kernel(z_ref, q_ref, k_ref, v_ref):
    def rows(block):
        return block.astype(jnp.float32).reshape(HALF, block.shape[-1]).astype(jnp.bfloat16)

    for h in range(z_ref.shape[1] // 2):
        left = h * GROUP * WIDTH
        q_ref[:, left : left + 2 * WIDTH] = rows(z_ref[:, 2 * h, :, : 2 * WIDTH])
        q_ref[:, left + 2 * WIDTH : left + 4 * WIDTH] = rows(z_ref[:, 2 * h + 1, :, : 2 * WIDTH])
        k_ref[:, h * WIDTH : (h + 1) * WIDTH] = rows(z_ref[:, 2 * h, :, 2 * WIDTH :])
        v_ref[:, h * WIDTH : (h + 1) * WIDTH] = rows(z_ref[:, 2 * h + 1, :, 2 * WIDTH :])


def place(z):
    groups, double, _, _ = z.shape
    heads = double // 2
    step = heads // PLACE_STEPS
    narrow = pl.BlockSpec((HALF, step * WIDTH), lambda h: (0, h))
    return pl.pallas_call(
        place_kernel,
        grid=(PLACE_STEPS,),
        in_specs=[pl.BlockSpec((groups, 2 * step, TILE, 3 * WIDTH), lambda h: (0, h, 0, 0))],
        out_specs=[pl.BlockSpec((HALF, step * GROUP * WIDTH), lambda h: (0, h)), narrow, narrow],
        out_shape=[
            jax.ShapeDtypeStruct((HALF, heads * GROUP * WIDTH), jnp.bfloat16),
            jax.ShapeDtypeStruct((HALF, heads * WIDTH), jnp.bfloat16),
            jax.ShapeDtypeStruct((HALF, heads * WIDTH), jnp.bfloat16),
        ],
        compiler_params=pltpu.CompilerParams(vmem_limit_bytes=32 * 1024 * 1024),
        name="place",
    )(z)


def per_device(queries, keys, values, grad_out, chosen_len, pack_of, pack_offset):
    pairs = lax.axis_size("dp") * lax.axis_size("slot")
    pair_here = lax.axis_index("dp") * lax.axis_size("slot") + lax.axis_index("slot")
    half_here = lax.axis_index("half").reshape(1)
    chosen_here = lax.dynamic_slice(chosen_len, (pair_here,), (1,))
    info = jnp.where(jnp.arange(16)[:, None] < 8, chosen_here[None], half_here[None])
    info = jnp.broadcast_to(info, (16, PAIR))

    heads = keys.shape[1] // WIDTH
    bounds = [0]
    for share in CHUNKS:
        bounds.append(bounds[-1] + share * heads // sum(CHUNKS))
    cuts = list(zip(bounds[:-1], bounds[1:]))
    owns = [
        jnp.concatenate([keys[:, lo * WIDTH : hi * WIDTH], values[:, lo * WIDTH : hi * WIDTH]], axis=1)
        for lo, hi in cuts
    ]
    firsts = [lax.ppermute(own, "half", [(0, 1)]) for own in owns]
    parts = []
    for (lo, hi), own, first in zip(cuts, owns, firsts):
        before = [parts[-1][0]] if parts else []
        dq, mine, part = attention(info, queries, grad_out, own, first, lo, hi, before)
        parts.append((dq, mine, lax.ppermute(part, "half", [(1, 0)])))
    pieces = combine(parts, heads)
    shape = pieces.shape
    piece = (pairs,) + shape[2:]
    spread = lax.all_to_all(pieces.reshape(piece), PAIRS_OVER, split_axis=0, concat_axis=0, tiled=True)
    ordered = reorder(pack_of, pack_offset, spread)
    gathered = lax.all_to_all(ordered, PAIRS_OVER, split_axis=0, concat_axis=0, tiled=True)
    return tuple(place(gathered.reshape(shape)))


def solution(mesh):
    shards, holders = mesh.devices.shape
    mesh = jax.sharding.Mesh(mesh.devices.reshape(shards, holders // 2, 2), ALL)
    rows = P(ALL, None)
    return jax.shard_map(
        per_device,
        mesh=mesh,
        in_specs=(rows, rows, rows, rows, P(), P(), P()),
        out_specs=(rows, rows, rows),
        check_vma=False,
    )
```

```python
import functools
import math

import jax
import jax.numpy as jnp
from jax import lax
from jax.experimental import pallas as pl
from jax.experimental.pallas import tpu as pltpu
from jax.sharding import PartitionSpec as P

WIDTH = 128
PAIR = 256
HALF = 128
GROUP = 4
CHUNKS = (3, 3, 2)
VMEM_ATT = 32
PLACE_STEPS = 2
TILE = 16
PAIRS_OVER = ("dp", "slot")
ALL = ("dp", "slot", "half")
CONTRACT_LAST = (((1,), (1,)), ((), ()))
CONTRACT_FIRST = (((0,), (0,)), ((), ()))


def four(ref, head):
    left = head * GROUP * WIDTH
    return jnp.concatenate([ref[:, left + i * WIDTH : left + (i + 1) * WIDTH] for i in range(GROUP)], axis=0)


def both(first_ref, own_ref, block):
    at = slice(block * WIDTH, (block + 1) * WIDTH)
    return jnp.concatenate([first_ref[:, at], own_ref[:, at]], axis=0)


def tiles(block):
    return block.reshape(HALF // TILE, TILE, WIDTH)


def score_kernel(lo, hi, info_ref, q_ref, g_ref, own_ref, first_ref, probs_ref, dscore_ref, part_ref):
    chosen = info_ref[0:1, :]
    second = info_ref[8:9, :]
    scale = 1.0 / math.sqrt(WIDTH)
    f32 = jnp.float32
    bf16 = jnp.bfloat16
    heads = hi - lo

    row = lax.broadcasted_iota(jnp.int32, (HALF, PAIR), 0) + HALF * second
    col = lax.broadcasted_iota(jnp.int32, (HALF, PAIR), 1) - HALF * (1 - second)
    low = jnp.where(row >= chosen, chosen, 0)
    allowed = (col >= low) & (col <= row)

    products = []
    for h in range(heads):
        keys, values = both(first_ref, own_ref, h), both(first_ref, own_ref, heads + h)
        scores = lax.dot_general(four(q_ref, lo + h), keys, CONTRACT_LAST, preferred_element_type=f32)
        dprob = lax.dot_general(four(g_ref, lo + h), values, CONTRACT_LAST, preferred_element_type=f32)
        products.append((scores, dprob))
    for h, (scores, dprob) in enumerate(products):
        scores = jnp.where(allowed[None], scores.reshape(GROUP, HALF, PAIR), -1e30).reshape(GROUP * HALF, PAIR)
        peak = jnp.max(scores, axis=1, keepdims=True)
        weights = jnp.exp2((scores - peak) * (scale * math.log2(math.e)))
        probs = weights * (1.0 / jnp.sum(weights, axis=1, keepdims=True))
        probs_b = probs.astype(bf16)
        delta = jnp.sum(probs_b.astype(f32) * dprob, axis=1, keepdims=True)
        dscore_b = (probs * (dprob - delta)).astype(bf16)
        probs_ref[h] = probs_b
        dscore_ref[h] = dscore_b
        q4, g4 = four(q_ref, lo + h), four(g_ref, lo + h)
        dk = lax.dot_general(dscore_b[:, :HALF], q4, CONTRACT_FIRST, preferred_element_type=f32) * scale
        dv = lax.dot_general(probs_b[:, :HALF], g4, CONTRACT_FIRST, preferred_element_type=f32)
        part_ref[:, 2 * h] = tiles(dk).astype(bf16)
        part_ref[:, 2 * h + 1] = tiles(dv).astype(bf16)


def gradient_kernel(lo, hi, probs_ref, dscore_ref, q_ref, g_ref, own_ref, first_ref, dq_ref, mine_ref):
    scale = 1.0 / math.sqrt(WIDTH)
    f32 = jnp.float32
    for h in range(hi - lo):
        dscore_b = dscore_ref[h]
        dq = jnp.dot(dscore_b, both(first_ref, own_ref, h), preferred_element_type=f32) * scale
        for i in range(GROUP):
            at = slice((i % 2) * WIDTH, (i % 2 + 1) * WIDTH)
            dq_ref[:, 2 * h + i // 2, :, at] = tiles(dq[i * HALF : (i + 1) * HALF]).astype(jnp.bfloat16)
        q4, g4 = four(q_ref, lo + h), four(g_ref, lo + h)
        dk = lax.dot_general(dscore_b[:, HALF:], q4, CONTRACT_FIRST, preferred_element_type=f32) * scale
        dv = lax.dot_general(probs_ref[h][:, HALF:], g4, CONTRACT_FIRST, preferred_element_type=f32)
        mine_ref[:, 2 * h] = tiles(dk)
        mine_ref[:, 2 * h + 1] = tiles(dv)


def whole(shape):
    return pl.BlockSpec(shape, lambda i, *_: (0,) * len(shape))


def in_order(kernel, name, operands, before, outs):
    def body(*refs):
        kernel(*refs[: len(operands)], *refs[len(operands) + len(before) :])

    return pl.pallas_call(
        body,
        grid=(1,),
        in_specs=[whole(a.shape) for a in operands] + [pl.BlockSpec(memory_space=pl.ANY)] * len(before),
        out_specs=[whole(a.shape) for a in outs],
        out_shape=outs,
        compiler_params=pltpu.CompilerParams(vmem_limit_bytes=VMEM_ATT * 1024 * 1024),
        name=name,
    )(*operands, *before)


def score(info, q, g, own, first, lo, hi, before):
    factor = jax.ShapeDtypeStruct((hi - lo, GROUP * HALF, PAIR), jnp.bfloat16)
    part = jax.ShapeDtypeStruct((HALF // TILE, 2 * (hi - lo), TILE, WIDTH), jnp.bfloat16)
    kernel = functools.partial(score_kernel, lo, hi)
    return in_order(kernel, f"score{lo}", (info, q, g, own, first), before, [factor, factor, part])


def gradient(probs, dscore, q, g, own, first, lo, hi, before):
    rows = (HALF // TILE, 2 * (hi - lo), TILE)
    outs = [jax.ShapeDtypeStruct(rows + (2 * WIDTH,), jnp.bfloat16), jax.ShapeDtypeStruct(rows + (WIDTH,), jnp.float32)]
    kernel = functools.partial(gradient_kernel, lo, hi)
    return in_order(kernel, f"gradient{lo}", (probs, dscore, q, g, own, first), before, outs)


def combine_kernel(*refs):
    x_ref = refs[-1]
    at = 0
    for c in range(len(refs) // 3):
        dq_ref, mine_ref, part_ref = refs[3 * c : 3 * c + 3]
        size = dq_ref.shape[1]
        total = mine_ref[...] + part_ref[...].astype(jnp.float32)
        x_ref[:, at : at + size, :, : 2 * WIDTH] = dq_ref[...]
        x_ref[:, at : at + size, :, 2 * WIDTH :] = total.astype(jnp.bfloat16)
        at += size


def combine(parts, heads):
    shape = (HALF // TILE, 2 * heads, TILE, 3 * WIDTH)
    operands = [a for part in parts for a in part]
    return pl.pallas_call(
        combine_kernel,
        grid=(1,),
        in_specs=[whole(a.shape) for a in operands],
        out_specs=whole(shape),
        out_shape=jax.ShapeDtypeStruct(shape, jnp.bfloat16),
        compiler_params=pltpu.CompilerParams(vmem_limit_bytes=16 * 1024 * 1024),
        name="combine",
    )(*operands)


def reorder_kernel(pack_of, pack_offset, y_ref, x_ref):
    def step(i, carry):
        block = pack_of[i] * (1024 // PAIR) + pack_offset[i] // PAIR
        x_ref[block] = y_ref[i]
        return carry

    lax.fori_loop(0, y_ref.shape[0], step, 0, unroll=32)


def reorder(pack_of, pack_offset, y):
    return pl.pallas_call(
        reorder_kernel,
        grid_spec=pltpu.PrefetchScalarGridSpec(
            num_scalar_prefetch=2, grid=(1,), in_specs=[whole(y.shape)], out_specs=whole(y.shape)
        ),
        out_shape=jax.ShapeDtypeStruct(y.shape, y.dtype),
        compiler_params=pltpu.CompilerParams(vmem_limit_bytes=16 * 1024 * 1024),
        name="reorder",
    )(pack_of, pack_offset, y)


def place_kernel(z_ref, q_ref, k_ref, v_ref):
    def rows(block):
        return block.astype(jnp.float32).reshape(HALF, block.shape[-1]).astype(jnp.bfloat16)

    for h in range(z_ref.shape[1] // 2):
        left = h * GROUP * WIDTH
        q_ref[:, left : left + 2 * WIDTH] = rows(z_ref[:, 2 * h, :, : 2 * WIDTH])
        q_ref[:, left + 2 * WIDTH : left + 4 * WIDTH] = rows(z_ref[:, 2 * h + 1, :, : 2 * WIDTH])
        k_ref[:, h * WIDTH : (h + 1) * WIDTH] = rows(z_ref[:, 2 * h, :, 2 * WIDTH :])
        v_ref[:, h * WIDTH : (h + 1) * WIDTH] = rows(z_ref[:, 2 * h + 1, :, 2 * WIDTH :])


def place(z):
    groups, double, _, _ = z.shape
    heads = double // 2
    step = heads // PLACE_STEPS
    narrow = pl.BlockSpec((HALF, step * WIDTH), lambda h: (0, h))
    return pl.pallas_call(
        place_kernel,
        grid=(PLACE_STEPS,),
        in_specs=[pl.BlockSpec((groups, 2 * step, TILE, 3 * WIDTH), lambda h: (0, h, 0, 0))],
        out_specs=[pl.BlockSpec((HALF, step * GROUP * WIDTH), lambda h: (0, h)), narrow, narrow],
        out_shape=[
            jax.ShapeDtypeStruct((HALF, heads * GROUP * WIDTH), jnp.bfloat16),
            jax.ShapeDtypeStruct((HALF, heads * WIDTH), jnp.bfloat16),
            jax.ShapeDtypeStruct((HALF, heads * WIDTH), jnp.bfloat16),
        ],
        compiler_params=pltpu.CompilerParams(vmem_limit_bytes=32 * 1024 * 1024),
        name="place",
    )(z)


def per_device(queries, keys, values, grad_out, chosen_len, pack_of, pack_offset):
    pairs = lax.axis_size("dp") * lax.axis_size("slot")
    pair_here = lax.axis_index("dp") * lax.axis_size("slot") + lax.axis_index("slot")
    half_here = lax.axis_index("half").reshape(1)
    chosen_here = lax.dynamic_slice(chosen_len, (pair_here,), (1,))
    info = jnp.where(jnp.arange(16)[:, None] < 8, chosen_here[None], half_here[None])
    info = jnp.broadcast_to(info, (16, PAIR))

    heads = keys.shape[1] // WIDTH
    bounds = [0]
    for share in CHUNKS:
        bounds.append(bounds[-1] + share * heads // sum(CHUNKS))
    cuts = list(zip(bounds[:-1], bounds[1:]))
    owns = [
        jnp.concatenate([keys[:, lo * WIDTH : hi * WIDTH], values[:, lo * WIDTH : hi * WIDTH]], axis=1)
        for lo, hi in cuts
    ]
    firsts = [lax.ppermute(own, "half", [(0, 1)]) for own in owns]
    factors, last = [], []
    for (lo, hi), own, first in zip(cuts, owns, firsts):
        probs, dscore, part = score(info, queries, grad_out, own, first, lo, hi, last)
        factors.append((probs, dscore, lax.ppermute(part, "half", [(1, 0)])))
        last = [dscore]
    parts = []
    for (lo, hi), own, first, (probs, dscore, part) in zip(cuts, owns, firsts, factors):
        dq, mine = gradient(probs, dscore, queries, grad_out, own, first, lo, hi, last)
        parts.append((dq, mine, part))
        last = [dq]
    pieces = combine(parts, heads)
    shape = pieces.shape
    piece = (pairs,) + shape[2:]
    spread = lax.all_to_all(pieces.reshape(piece), PAIRS_OVER, split_axis=0, concat_axis=0, tiled=True)
    ordered = reorder(pack_of, pack_offset, spread)
    gathered = lax.all_to_all(ordered, PAIRS_OVER, split_axis=0, concat_axis=0, tiled=True)
    return tuple(place(gathered.reshape(shape)))


def solution(mesh):
    shards, holders = mesh.devices.shape
    mesh = jax.sharding.Mesh(mesh.devices.reshape(shards, holders // 2, 2), ALL)
    rows = P(ALL, None)
    return jax.shard_map(
        per_device,
        mesh=mesh,
        in_specs=(rows, rows, rows, rows, P(), P(), P()),
        out_specs=(rows, rows, rows),
        check_vma=False,
    )
```

```python
import functools
import math

import jax
import jax.numpy as jnp
from jax import lax
from jax.experimental import pallas as pl
from jax.experimental.pallas import tpu as pltpu
from jax.sharding import PartitionSpec as P

WIDTH = 128
PAIR = 256
HALF = 128
GROUP = 4
CHUNKS = (3, 3, 2)
VMEM_ATT = 32
PLACE_STEPS = 1
TILE = 16
PAIRS_OVER = ("dp", "slot")
ALL = ("dp", "slot", "half")
CONTRACT_LAST = (((1,), (1,)), ((), ()))
CONTRACT_FIRST = (((0,), (0,)), ((), ()))


def four(ref, head):
    left = head * GROUP * WIDTH
    return jnp.concatenate([ref[:, left + i * WIDTH : left + (i + 1) * WIDTH] for i in range(GROUP)], axis=0)


def both(first_ref, own_ref, block):
    at = slice(block * WIDTH, (block + 1) * WIDTH)
    return jnp.concatenate([first_ref[:, at], own_ref[:, at]], axis=0)


def tiles(block):
    return block.reshape(HALF // TILE, TILE, WIDTH)


def score_kernel(lo, hi, info_ref, q_ref, g_ref, own_ref, first_ref, probs_ref, dscore_ref, part_ref):
    chosen = info_ref[0:1, :]
    second = info_ref[8:9, :]
    scale = 1.0 / math.sqrt(WIDTH)
    f32 = jnp.float32
    bf16 = jnp.bfloat16
    heads = hi - lo

    row = lax.broadcasted_iota(jnp.int32, (HALF, PAIR), 0) + HALF * second
    col = lax.broadcasted_iota(jnp.int32, (HALF, PAIR), 1) - HALF * (1 - second)
    low = jnp.where(row >= chosen, chosen, 0)
    allowed = (col >= low) & (col <= row)

    products = []
    for h in range(heads):
        keys, values = both(first_ref, own_ref, h), both(first_ref, own_ref, heads + h)
        scores = lax.dot_general(four(q_ref, lo + h), keys, CONTRACT_LAST, preferred_element_type=f32)
        dprob = lax.dot_general(four(g_ref, lo + h), values, CONTRACT_LAST, preferred_element_type=f32)
        products.append((scores, dprob))
    for h, (scores, dprob) in enumerate(products):
        scores = jnp.where(allowed[None], scores.reshape(GROUP, HALF, PAIR), -1e30).reshape(GROUP * HALF, PAIR)
        peak = jnp.max(scores, axis=1, keepdims=True)
        weights = jnp.exp2((scores - peak) * (scale * math.log2(math.e)))
        probs = weights * (1.0 / jnp.sum(weights, axis=1, keepdims=True))
        probs_b = probs.astype(bf16)
        delta = jnp.sum(probs_b.astype(f32) * dprob, axis=1, keepdims=True)
        dscore_b = (probs * (dprob - delta)).astype(bf16)
        probs_ref[h] = probs_b
        dscore_ref[h] = dscore_b
        q4, g4 = four(q_ref, lo + h), four(g_ref, lo + h)
        dk = lax.dot_general(dscore_b[:, :HALF], q4, CONTRACT_FIRST, preferred_element_type=f32) * scale
        dv = lax.dot_general(probs_b[:, :HALF], g4, CONTRACT_FIRST, preferred_element_type=f32)
        part_ref[:, 2 * h] = tiles(dk).astype(bf16)
        part_ref[:, 2 * h + 1] = tiles(dv).astype(bf16)


def gradient_kernel(lo, hi, probs_ref, dscore_ref, q_ref, g_ref, own_ref, first_ref, dq_ref, mine_ref):
    scale = 1.0 / math.sqrt(WIDTH)
    f32 = jnp.float32
    for h in range(hi - lo):
        dscore_b = dscore_ref[h]
        dq = jnp.dot(dscore_b, both(first_ref, own_ref, h), preferred_element_type=f32) * scale
        for i in range(GROUP):
            at = slice((i % 2) * WIDTH, (i % 2 + 1) * WIDTH)
            dq_ref[:, 2 * h + i // 2, :, at] = tiles(dq[i * HALF : (i + 1) * HALF]).astype(jnp.bfloat16)
        q4, g4 = four(q_ref, lo + h), four(g_ref, lo + h)
        dk = lax.dot_general(dscore_b[:, HALF:], q4, CONTRACT_FIRST, preferred_element_type=f32) * scale
        dv = lax.dot_general(probs_ref[h][:, HALF:], g4, CONTRACT_FIRST, preferred_element_type=f32)
        mine_ref[:, 2 * h] = tiles(dk)
        mine_ref[:, 2 * h + 1] = tiles(dv)


def whole(shape):
    return pl.BlockSpec(shape, lambda i, *_: (0,) * len(shape))


def in_order(kernel, name, operands, before, outs):
    def body(*refs):
        kernel(*refs[: len(operands)], *refs[len(operands) + len(before) :])

    return pl.pallas_call(
        body,
        grid=(1,),
        in_specs=[whole(a.shape) for a in operands] + [pl.BlockSpec(memory_space=pl.ANY)] * len(before),
        out_specs=[whole(a.shape) for a in outs],
        out_shape=outs,
        compiler_params=pltpu.CompilerParams(vmem_limit_bytes=VMEM_ATT * 1024 * 1024),
        name=name,
    )(*operands, *before)


def score(info, q, g, own, first, lo, hi, before):
    factor = jax.ShapeDtypeStruct((hi - lo, GROUP * HALF, PAIR), jnp.bfloat16)
    part = jax.ShapeDtypeStruct((HALF // TILE, 2 * (hi - lo), TILE, WIDTH), jnp.bfloat16)
    kernel = functools.partial(score_kernel, lo, hi)
    return in_order(kernel, f"score{lo}", (info, q, g, own, first), before, [factor, factor, part])


def gradient(probs, dscore, q, g, own, first, lo, hi, before):
    rows = (HALF // TILE, 2 * (hi - lo), TILE)
    outs = [jax.ShapeDtypeStruct(rows + (2 * WIDTH,), jnp.bfloat16), jax.ShapeDtypeStruct(rows + (WIDTH,), jnp.float32)]
    kernel = functools.partial(gradient_kernel, lo, hi)
    return in_order(kernel, f"gradient{lo}", (probs, dscore, q, g, own, first), before, outs)


def combine_kernel(*refs):
    x_ref = refs[-1]
    at = 0
    for c in range(len(refs) // 3):
        dq_ref, mine_ref, part_ref = refs[3 * c : 3 * c + 3]
        size = dq_ref.shape[1]
        total = mine_ref[...] + part_ref[...].astype(jnp.float32)
        x_ref[:, at : at + size, :, : 2 * WIDTH] = dq_ref[...]
        x_ref[:, at : at + size, :, 2 * WIDTH :] = total.astype(jnp.bfloat16)
        at += size


def combine(parts, heads):
    shape = (HALF // TILE, 2 * heads, TILE, 3 * WIDTH)
    operands = [a for part in parts for a in part]
    return pl.pallas_call(
        combine_kernel,
        grid=(1,),
        in_specs=[whole(a.shape) for a in operands],
        out_specs=whole(shape),
        out_shape=jax.ShapeDtypeStruct(shape, jnp.bfloat16),
        compiler_params=pltpu.CompilerParams(vmem_limit_bytes=16 * 1024 * 1024),
        name="combine",
    )(*operands)


def reorder_kernel(pack_of, pack_offset, y_ref, x_ref):
    def step(i, carry):
        block = pack_of[i] * (1024 // PAIR) + pack_offset[i] // PAIR
        x_ref[block] = y_ref[i]
        return carry

    lax.fori_loop(0, y_ref.shape[0], step, 0, unroll=32)


def reorder(pack_of, pack_offset, y):
    return pl.pallas_call(
        reorder_kernel,
        grid_spec=pltpu.PrefetchScalarGridSpec(
            num_scalar_prefetch=2, grid=(1,), in_specs=[whole(y.shape)], out_specs=whole(y.shape)
        ),
        out_shape=jax.ShapeDtypeStruct(y.shape, y.dtype),
        compiler_params=pltpu.CompilerParams(vmem_limit_bytes=16 * 1024 * 1024),
        name="reorder",
    )(pack_of, pack_offset, y)


def place_kernel(z_ref, q_ref, k_ref, v_ref):
    def rows(block):
        return block.astype(jnp.float32).reshape(HALF, block.shape[-1]).astype(jnp.bfloat16)

    for h in range(z_ref.shape[1] // 2):
        left = h * GROUP * WIDTH
        q_ref[:, left : left + 2 * WIDTH] = rows(z_ref[:, 2 * h, :, : 2 * WIDTH])
        q_ref[:, left + 2 * WIDTH : left + 4 * WIDTH] = rows(z_ref[:, 2 * h + 1, :, : 2 * WIDTH])
        k_ref[:, h * WIDTH : (h + 1) * WIDTH] = rows(z_ref[:, 2 * h, :, 2 * WIDTH :])
        v_ref[:, h * WIDTH : (h + 1) * WIDTH] = rows(z_ref[:, 2 * h + 1, :, 2 * WIDTH :])


def place(z):
    groups, double, _, _ = z.shape
    heads = double // 2
    step = heads // PLACE_STEPS
    narrow = pl.BlockSpec((HALF, step * WIDTH), lambda h: (0, h))
    return pl.pallas_call(
        place_kernel,
        grid=(PLACE_STEPS,),
        in_specs=[pl.BlockSpec((groups, 2 * step, TILE, 3 * WIDTH), lambda h: (0, h, 0, 0))],
        out_specs=[pl.BlockSpec((HALF, step * GROUP * WIDTH), lambda h: (0, h)), narrow, narrow],
        out_shape=[
            jax.ShapeDtypeStruct((HALF, heads * GROUP * WIDTH), jnp.bfloat16),
            jax.ShapeDtypeStruct((HALF, heads * WIDTH), jnp.bfloat16),
            jax.ShapeDtypeStruct((HALF, heads * WIDTH), jnp.bfloat16),
        ],
        compiler_params=pltpu.CompilerParams(vmem_limit_bytes=32 * 1024 * 1024),
        name="place",
    )(z)


def per_device(queries, keys, values, grad_out, chosen_len, pack_of, pack_offset):
    pairs = lax.axis_size("dp") * lax.axis_size("slot")
    pair_here = lax.axis_index("dp") * lax.axis_size("slot") + lax.axis_index("slot")
    half_here = lax.axis_index("half").reshape(1)
    chosen_here = lax.dynamic_slice(chosen_len, (pair_here,), (1,))
    info = jnp.where(jnp.arange(16)[:, None] < 8, chosen_here[None], half_here[None])
    info = jnp.broadcast_to(info, (16, PAIR))

    heads = keys.shape[1] // WIDTH
    bounds = [0]
    for share in CHUNKS:
        bounds.append(bounds[-1] + share * heads // sum(CHUNKS))
    cuts = list(zip(bounds[:-1], bounds[1:]))
    owns = [
        jnp.concatenate([keys[:, lo * WIDTH : hi * WIDTH], values[:, lo * WIDTH : hi * WIDTH]], axis=1)
        for lo, hi in cuts
    ]
    firsts = [lax.ppermute(own, "half", [(0, 1)]) for own in owns]
    factors, last = [], []
    for (lo, hi), own, first in zip(cuts, owns, firsts):
        probs, dscore, part = score(info, queries, grad_out, own, first, lo, hi, last)
        factors.append((probs, dscore, lax.ppermute(part, "half", [(1, 0)])))
        last = [dscore]
    parts = []
    for (lo, hi), own, first, (probs, dscore, part) in zip(cuts, owns, firsts, factors):
        dq, mine = gradient(probs, dscore, queries, grad_out, own, first, lo, hi, last)
        parts.append((dq, mine, part))
        last = [dq]
    pieces = combine(parts, heads)
    shape = pieces.shape
    piece = (pairs,) + shape[2:]
    spread = lax.all_to_all(pieces.reshape(piece), PAIRS_OVER, split_axis=0, concat_axis=0, tiled=True)
    ordered = reorder(pack_of, pack_offset, spread)
    gathered = lax.all_to_all(ordered, PAIRS_OVER, split_axis=0, concat_axis=0, tiled=True)
    return tuple(place(gathered.reshape(shape)))


def solution(mesh):
    shards, holders = mesh.devices.shape
    mesh = jax.sharding.Mesh(mesh.devices.reshape(shards, holders // 2, 2), ALL)
    rows = P(ALL, None)
    return jax.shard_map(
        per_device,
        mesh=mesh,
        in_specs=(rows, rows, rows, rows, P(), P(), P()),
        out_specs=(rows, rows, rows),
        check_vma=False,
    )
```
